256 devices in a mesh: batch: 4 (over y_lo, core), seq: 64 (over z, x, y_hi).
Axes of the slice: x: 4, y: 4 (y_hi: 2, y_lo: 2; y = y_hi * 2 + y_lo), z: 8, core: 2. Of those that a mesh axis runs over, the one named last changes fastest.
Arguments:
- queries: bfloat16 [65536, 1024], P(('batch', 'seq')), parts along dimension 0, may hold values from -6 to 6
- keys: bfloat16 [65536, 1024], P(('batch', 'seq')), parts along dimension 0, may hold values from -6 to 6
- values: bfloat16 [65536, 1024], P(('batch', 'seq')), parts along dimension 0, may hold values from -6 to 6
- out_weight: bfloat16 [1024, 1024], replicated, may hold values from -0.1875 to 0.1875
Outputs:
- output: bfloat16 [65536, 1024], P(('batch', 'seq')), parts along dimension 0
The draws below stay inside these ranges and needn't reach their ends.
There are 4 independent parts, one for each index of `batch`. The reference program is written for one: setup_inputs(seed, part) draws one part's arguments, and reference() takes and returns one part's arrays. A program takes and returns all parts, laid end to end along the dimension named above; an argument that names none is the same for every part. Nothing has to cross between parts.
All inputs are finite; a program needn't handle non-finite values.
Results may differ from the reference program's by a relative error of at most 0.011.
Values may be sent and summed in bfloat16 or wider, within the bound.
A program may use at most 64 MiB of HBM per device.

```python
import math
import jax
import jax.numpy as jnp
from jax import lax

HEADS = 16
HEAD = 64
D = 1024
BLOCK = 128
TOKENS = 16384


def level_shapes():
    depth_count = (TOKENS // BLOCK).bit_length() - 1
    return [(TOKENS // 2 ** section, 2 ** section) for section in range(depth_count)]


def piece_weights(count):
    base = 1.0 / math.sqrt(count)
    return [1.2 if section >= count - 2 else base for section in range(count)]


def spread_sum(pieces, shapes):
    weight_list = piece_weights(len(shapes))
    field = jnp.zeros((TOKENS, D), jnp.float32)
    for piece, weight_each, (row_count, span) in zip(pieces, weight_list, shapes):
        field = field + weight_each * jnp.broadcast_to(piece[:, None, :], (row_count, span, D)).reshape(TOKENS, D)
    return field


def normal_pieces(key, shapes):
    return [jnp.clip(jax.random.normal(jax.random.fold_in(key, index), (row_count, D), jnp.float32), -6.0, 6.0) for index, (row_count, span) in enumerate(shapes)]


def draw_queries(key, part):
    key = jax.random.fold_in(key, 1)
    shapes = level_shapes()
    field = jnp.clip(spread_sum(normal_pieces(key, shapes), shapes), -6.0, 6.0)
    return field.astype(jnp.bfloat16)


def draw_keys(key, part):
    key = jax.random.fold_in(key, 2)
    shapes = level_shapes()
    field = jnp.clip(spread_sum(normal_pieces(key, shapes), shapes), -6.0, 6.0)
    return field.astype(jnp.bfloat16)


def draw_values(key, part):
    key = jax.random.fold_in(key, 3)
    shapes = level_shapes()
    field = jnp.clip(spread_sum(normal_pieces(key, shapes), shapes), -6.0, 6.0)
    return field.astype(jnp.bfloat16)


def gaussian(own_key, dims, deviation, reach, held_as=jnp.bfloat16):
    return jnp.clip(deviation * jax.random.normal(own_key, dims, jnp.float32), -reach, reach).astype(held_as)


def setup_inputs(seed: int = 0, part: int = 0) -> dict:
    key_of = jax.random.split(jax.random.key(seed), 5)
    part_splits = jax.random.split(jax.random.fold_in(key_of[4], part), 5)
    return {
        "queries": draw_queries(jax.random.fold_in(jax.random.fold_in(key_of[4], part), 71), part),
        "keys": draw_keys(jax.random.fold_in(jax.random.fold_in(key_of[4], part), 71), part),
        "values": draw_values(jax.random.fold_in(jax.random.fold_in(key_of[4], part), 71), part),
        "out_weight": gaussian(key_of[3], (D, D), D ** -0.5, 0.1875),
    }


masked_score = -1e+30

def coarsen(coarse_in):
    in_shape = coarse_in.shape
    paired = coarse_in.reshape(in_shape[:-2] + (in_shape[-2] // 2, 2, in_shape[-1])).astype(jnp.float32)
    return ((paired[..., 0, :] + paired[..., 1, :]) * 0.5).astype(jnp.bfloat16)

def one_block(query_rows, key_rows, value_rows, valid_keys):
    row_count = query_rows.shape[0]
    col_count = key_rows.shape[0]
    query_heads = query_rows.astype(jnp.float32).reshape(row_count, HEADS, HEAD)
    key_heads = key_rows.astype(jnp.float32).reshape(col_count, HEADS, HEAD)
    value_heads = value_rows.astype(jnp.float32).reshape(col_count, HEADS, HEAD)
    scores = jnp.einsum('qhe,khe->hqk', query_heads, key_heads) * (1.0 / math.sqrt(HEAD))
    scores = jnp.where(valid_keys[None, None, :], scores, masked_score)
    peak_row = lax.optimization_barrier(jnp.max(scores, axis=2))
    weights = jnp.exp(scores - peak_row[:, :, None])
    totals = lax.optimization_barrier(jnp.sum(weights, axis=2))
    rounded = lax.optimization_barrier(weights.astype(jnp.bfloat16)).astype(jnp.float32)
    summary = jnp.einsum('hqk,khe->qhe', rounded, value_heads)
    return (peak_row.T, totals.T, summary)

def level_zero(queries, keys, values):
    length, features = keys.shape
    blocks = length // BLOCK
    padding = jnp.zeros((BLOCK, features), jnp.bfloat16)
    key_pad = jnp.concatenate((padding, keys, padding), axis=0)
    value_pad = jnp.concatenate((padding, values, padding), axis=0)
    columns = jnp.arange(3 * BLOCK, dtype=jnp.int32)

    def visit(block_index):
        start = (block_index * BLOCK).astype(jnp.int32)
        query_rows = lax.dynamic_slice_in_dim(queries, start, BLOCK, 0)
        key_rows = lax.dynamic_slice_in_dim(key_pad, start, 3 * BLOCK, 0)
        value_rows = lax.dynamic_slice_in_dim(value_pad, start, 3 * BLOCK, 0)
        position = start + columns
        valid_keys = (position >= BLOCK) & (position < length + BLOCK)
        return one_block(query_rows, key_rows, value_rows, valid_keys)
    peak_row, totals, summary = lax.map(visit, jnp.arange(blocks, dtype=jnp.int32))
    return (peak_row.reshape(length, HEADS), totals.reshape(length, HEADS), summary.reshape(length, HEADS, HEAD))

def sibling_level(coarse_query, coarse_key, coarse_value):
    row_count, features = coarse_query.shape
    blocks = row_count // BLOCK
    query_blocks = coarse_query.reshape(blocks, BLOCK, features)
    key_blocks = coarse_key.reshape(blocks // 2, 2, BLOCK, features)[:, ::-1].reshape(blocks, BLOCK, features)
    value_blocks = coarse_value.reshape(blocks // 2, 2, BLOCK, features)[:, ::-1].reshape(blocks, BLOCK, features)
    valid_keys = jnp.ones((BLOCK,), dtype=bool)

    def visit(blocks_in):
        return one_block(blocks_in[0], blocks_in[1], blocks_in[2], valid_keys)
    peak_row, totals, summary = lax.map(visit, (query_blocks, key_blocks, value_blocks))
    return (peak_row.reshape(row_count, HEADS), totals.reshape(row_count, HEADS), summary.reshape(row_count, HEADS, HEAD))

def combine(results, length):
    peak_all = jnp.full((length, HEADS), masked_score, jnp.float32)
    for peak_row, totals, summary in results:
        row_count = peak_row.shape[0]
        factor = length // row_count
        spread = jnp.broadcast_to(peak_row[:, None, :], (row_count, factor, HEADS)).reshape(length, HEADS)
        peak_all = jnp.maximum(peak_all, spread)
    mass_all = jnp.zeros((length, HEADS), jnp.float32)
    summary_all = jnp.zeros((length, HEADS, HEAD), jnp.float32)
    for peak_row, totals, summary in results:
        row_count = peak_row.shape[0]
        factor = length // row_count
        rescale = jnp.exp(peak_row[:, None, :] - peak_all.reshape(row_count, factor, HEADS))
        mass_all = mass_all + (rescale * totals[:, None, :]).reshape(length, HEADS)
        summary_all = summary_all + (rescale[..., None] * summary[:, None]).reshape(length, HEADS, HEAD)
    return (summary_all / mass_all[..., None]).astype(jnp.bfloat16).reshape(length, HEADS * HEAD)

def reference(queries, keys, values, out_weight):
    length = queries.shape[0]
    top_level = (length // BLOCK).bit_length() - 2
    results = [level_zero(queries, keys, values)]
    coarse_query, coarse_key, coarse_value = (queries, keys, values)
    for section_level in range(1, top_level + 1):
        coarse_query = coarsen(coarse_query)
        coarse_key = coarsen(coarse_key)
        coarse_value = coarsen(coarse_value)
        results.append(sibling_level(coarse_query, coarse_key, coarse_value))
    attended = combine(results, length)
    return jnp.dot(attended, out_weight, preferred_element_type=jnp.float32).astype(jnp.bfloat16)
```

```python
import math

import jax
import jax.numpy as jnp
from jax import lax
from jax.experimental import pallas as pl
from jax.experimental.pallas import tpu as pltpu
from jax.sharding import PartitionSpec as P

MESH = pl.DeviceIdType.MESH
ROWS = 256
BLOCK = 128
D = 1024
HALF = 512
LANES = 128
CHUNKS = 4
FACTOR = math.log2(math.e) / 8.0
BF, F32 = jnp.bfloat16, jnp.float32
MASKED = -1e30


def averaging(rows):
    i = lax.broadcasted_iota(jnp.int32, (rows // 2, rows), 0)
    j = lax.broadcasted_iota(jnp.int32, (rows // 2, rows), 1)
    return jnp.where((j == 2 * i) | (j == 2 * i + 1), 0.5, 0.0).astype(BF)


def coarsen(x):
    rows = x.shape[0]
    if rows > 256:
        return jnp.concatenate([coarsen(x[i : i + 256]) for i in range(0, rows, 256)], axis=0)
    return jnp.dot(averaging(rows), x, preferred_element_type=F32).astype(BF)


def low_lanes(rows):
    return lax.broadcasted_iota(jnp.int32, (rows, LANES), 1) < 64


def split_keys(k):
    low, zero = low_lanes(k.shape[0]), jnp.zeros_like(k)
    return jnp.where(low, k, zero), jnp.where(low, zero, k)


def split_values(v):
    low, zero, one = low_lanes(v.shape[0]), jnp.zeros_like(v), jnp.ones_like(v)
    return (
        jnp.concatenate([jnp.where(low, v, zero), jnp.where(low, one, zero)], axis=1),
        jnp.concatenate([jnp.where(low, zero, v), jnp.where(low, zero, one)], axis=1),
    )


def attend(q, keys, values, masks=()):
    weights, peaks = [], []
    for k in keys:
        s = lax.dot_general(q, k, (((1,), (1,)), ((), ())), preferred_element_type=F32)
        for first, last, hidden in masks:
            parts = [s[:, :first], jnp.where(hidden, MASKED, s[:, first:last]), s[:, last:]]
            s = jnp.concatenate([part for part in parts if part.shape[1]], axis=1)
        peak = jnp.max(s, axis=1, keepdims=True)
        weights.append(jnp.exp2((s - peak) * FACTOR).astype(BF))
        peaks.append(peak * FACTOR)
    total = jnp.dot(
        jnp.concatenate(weights, axis=1), jnp.concatenate(values, axis=0), preferred_element_type=F32
    )
    peak = jnp.where(low_lanes(q.shape[0]), peaks[0], peaks[1])
    return peak, total[:, LANES:], total[:, :LANES]


def merge(a, b):
    peak = jnp.maximum(a[0], b[0])
    scale_a, scale_b = jnp.exp2(a[0] - peak), jnp.exp2(b[0] - peak)
    return peak, scale_a * a[1] + scale_b * b[1], scale_a * a[2] + scale_b * b[2]


def kernel(q_hbm, k_hbm, v_hbm, w_hbm, out_ref, *scratch):
    (own, qp, kx, vx, wv, st4, r4, z4s, z5s, z6s, z4r, z5r, z6r, cos, cor, s2, r2, s3, r3, ab, ret, acc, rep,
     own_sem, pair_sem, w_sem, e1s, e1r, nats, natr, rels, relr, s2s, s2r, s3s, s3r, a2as, a2ar, zs, zr, cs, cr,
     rs, rr, self_sem) = scratch
    b, s = lax.axis_index("batch"), lax.axis_index("seq")
    h, x, z, p = s % 2, (s // 2) % 4, s // 8, s // 2
    me8 = s % 8
    partner = (b, p * 2 + 1 - h)

    def pair(index):
        return (b, ((index + 32) % 32) * 2 + h)

    def in_plane(x2):
        return (b, z * 8 + x2 * 2 + h)

    def along_z(z2):
        return (b, z2 * 8 + me8)

    def flip(v, bits):
        for bit in (1, 2, 4):
            if bits & bit:
                v = v + bit - 2 * bit * ((v // bit) % 2)
        return v

    def remote(src, dst, ssem, rsem, target):
        return pltpu.make_async_remote_copy(
            src_ref=src, dst_ref=dst, send_sem=ssem, recv_sem=rsem, device_id=target, device_id_type=MESH
        )

    sent = []

    def send(*args):
        copy = remote(*args)
        copy.start()
        sent.append(copy)

    def received(dst, ssem, rsem):
        remote(dst, dst, ssem, rsem, partner).wait_recv()

    barrier = pltpu.get_barrier_semaphore()
    targets = [(b, z * 8 + (me8 + j) % 8) for j in range(1, 8)]
    targets += [along_z((z + j) % 8) for j in range(1, 8)]
    targets += [pair(p + 1), pair(p - 1)]
    for target in targets:
        pl.semaphore_signal(barrier, inc=1, device_id=target, device_id_type=MESH)

    inputs = (q_hbm, k_hbm, v_hbm)
    own_copies = [pltpu.make_async_copy(inputs[i], own.at[i], own_sem.at[i]) for i in range(3)]
    for copy in own_copies:
        copy.start()

    def mine(c):
        return pl.ds(pl.multiple_of(h * HALF + c * LANES, LANES), LANES)

    def theirs(c):
        return pl.ds(pl.multiple_of((1 - h) * HALF + c * LANES, LANES), LANES)

    def at(start, size):
        return pl.ds(pl.multiple_of(start, 128), size)

    pair_refs = (qp, kx, vx)
    offsets = (0, BLOCK, BLOCK)
    pair_copies = []
    for c in range(CHUNKS):
        for i in range(3):
            copy = pltpu.make_async_copy(
                inputs[i].at[:, mine(c)], pair_refs[i].at[c, at(offsets[i] + ROWS * h, ROWS)], pair_sem.at[c, i]
            )
            copy.start()
            pair_copies.append(copy)
    w_copy = pltpu.make_async_copy(w_hbm, wv, w_sem)
    w_copy.start()

    for i in range(3):
        own_copies[i].wait()
        coarse = own[i]
        for _ in range(4):
            coarse = coarsen(coarse)
        for hp in range(8):
            st4[(hp % 4) * 2 + hp // 4, i] = coarse[:, hp * LANES : (hp + 1) * LANES]

    pl.semaphore_wait(barrier, len(targets))

    for j in range(1, 8):
        t = (me8 + j) % 8
        send(st4.at[t], r4.at[:, pl.ds(pl.multiple_of(me8 * 16, 16), 16)], a2as.at[t], a2ar.at[me8], (b, z * 8 + t))
    self_copy = pltpu.make_async_copy(st4.at[me8], r4.at[:, pl.ds(pl.multiple_of(me8 * 16, 16), 16)], self_sem)
    self_copy.start()

    def exchange(c, i):
        send(
            inputs[i].at[:, theirs(c)],
            pair_refs[i].at[c, at(offsets[i] + ROWS * h, ROWS)],
            e1s.at[c, i],
            e1r.at[c, i],
            partner,
        )

    def exchanged(c, i):
        received(pair_refs[i].at[c, at(offsets[i] + ROWS * (1 - h), ROWS)], e1s.at[c, i], e1r.at[c, i])

    for c, i in ((0, 1), (0, 2), (1, 1), (1, 2), (0, 0), (2, 1), (2, 2), (1, 0), (3, 1), (3, 2), (2, 0), (3, 0)):
        exchange(c, i)

    native_target = pair(p - 1 + 2 * h)
    relay_target = pair(p + 1 - 2 * h)
    for c in range(CHUNKS):
        for i in (1, 2):
            send(
                inputs[i].at[at(BLOCK * h, BLOCK), mine(c)],
                pair_refs[i].at[c, at(640 * (1 - h), BLOCK)],
                nats.at[c, i - 1],
                natr.at[c, i - 1],
                native_target,
            )

    def spread(c):
        for i in (1, 2):
            pair_copies[c * 3 + i].wait()
            exchanged(c, i)
            send(
                pair_refs[i].at[c, at(BLOCK * (4 - 3 * h), BLOCK)],
                pair_refs[i].at[c, at(640 * h, BLOCK)],
                rels.at[c, i - 1],
                relr.at[c, i - 1],
                relay_target,
            )
            level2 = coarsen(coarsen(pair_refs[i][c, BLOCK : BLOCK + 512]))
            s2[c, i - 1] = level2
            s3[c, i - 1] = coarsen(level2)
        send(s2.at[c], r2.at[c], s2s.at[c], s2r.at[c], in_plane(flip(x, 1)))
        for k in (0, 1):
            send(
                s3.at[c], r3.at[c, :, pl.ds(64 * k, 64)], s3s.at[c, k], s3r.at[c, k], in_plane(flip(x, 2 + k))
            )

    def coarse_spread():
        self_copy.wait()
        for j in range(1, 8):
            t = (me8 + j) % 8
            received(r4.at[:, pl.ds(pl.multiple_of(t * 16, 16), 16)], a2as.at[t], a2ar.at[t])
        for i in (1, 2):
            level4 = r4[i]
            level5 = coarsen(level4)
            z4s[i - 1] = level4
            z5s[i - 1] = level5
            z6s[i - 1] = coarsen(level5)
        send(z4s, z4r, zs.at[0], zr.at[0], along_z(flip(z, 1)))
        for k in range(2):
            send(z5s, z5r.at[:, pl.ds(64 * k, 64)], zs.at[1 + k], zr.at[1 + k], along_z(flip(z, 2 + k)))
        for k in range(4):
            send(z6s, z6r.at[:, pl.ds(32 * k, 32)], zs.at[3 + k], zr.at[3 + k], along_z(flip(z, 4 + k)))

    def repeated(level):
        rows = level[0].shape[0]
        for i in range(3):
            rep[i, pl.ds(0, rows, stride=2), :] = level[i]
            rep[i, pl.ds(1, rows, stride=2), :] = level[i]
        return tuple(rep[i, : 2 * rows, :] for i in range(3))

    def coarse_attend():
        received(z4r, zs.at[0], zr.at[0])
        for k in range(2):
            received(z5r.at[:, pl.ds(64 * k, 64)], zs.at[1 + k], zr.at[1 + k])
        for k in range(4):
            received(z6r.at[:, pl.ds(32 * k, 32)], zs.at[3 + k], zr.at[3 + k])
        q4 = r4[0]
        q5 = coarsen(q4)
        q6 = coarsen(q5)
        level = attend(q6, split_keys(z6r[0]), split_values(z6r[1]))
        level = merge(repeated(level), attend(q5, split_keys(z5r[0]), split_values(z5r[1])))
        level = merge(repeated(level), attend(q4, split_keys(z4r[0]), split_values(z4r[1])))
        for i in range(3):
            for x2 in range(4):
                cos[x2, i] = level[i][x2 * 32 : x2 * 32 + 32]
        for j in range(1, 4):
            x2 = (x + j) % 4
            send(cos.at[x2], cor.at[x], cs.at[x2], cr.at[x], in_plane(x2))
        local = pltpu.make_async_copy(cos.at[x], cor.at[x], self_sem)
        local.start()
        local.wait()

    def coarse_received():
        for j in range(1, 4):
            x2 = (x + j) % 4
            received(cor.at[x2], cs.at[x2], cr.at[x2])

    def compute(c):
        pair_copies[c * 3].wait()
        exchanged(c, 0)
        q0 = qp[c]
        q1 = coarsen(q0)
        q2 = coarsen(q1)
        q3 = coarsen(q2)
        for k in (0, 1):
            received(r3.at[c, :, pl.ds(64 * k, 64)], s3s.at[c, k], s3r.at[c, k])
        level = tuple(cor[c, i] for i in range(3))
        level = merge(repeated(level), attend(q3, split_keys(r3[c, 0]), split_values(r3[c, 1])))
        received(r2.at[c], s2s.at[c], s2r.at[c])
        level = merge(repeated(level), attend(q2, split_keys(r2[c, 0]), split_values(r2[c, 1])))
        k1 = split_keys(coarsen(kx[c, BLOCK : BLOCK + 512]))
        v1 = split_values(coarsen(vx[c, BLOCK : BLOCK + 512]))
        parts = []
        for block in (0, 1):
            other = slice(128 * (1 - block), 128 * (2 - block))
            parts.append(attend(q1[128 * block : 128 * block + 128], [k[other] for k in k1], [v[other] for v in v1]))
        fine = tuple(jnp.concatenate([part[i] for part in parts], axis=0) for i in range(3))
        level = repeated(merge(repeated(level), fine))
        for i in (1, 2):
            received(pair_refs[i].at[c, at(640 * (1 - h), BLOCK)], nats.at[c, i - 1], natr.at[c, i - 1])
            received(pair_refs[i].at[c, at(640 * h, BLOCK)], rels.at[c, i - 1], relr.at[c, i - 1])
        k0 = split_keys(kx[c])
        v0 = split_values(vx[c])
        for block in range(4):
            window = slice(128 * block, 128 * block + 384)
            rows = slice(128 * block, 128 * block + 128)
            masks = ()
            if block == 0:
                masks = ((0, 128, p == 0),)
            if block == 3:
                masks = ((256, 384, p == 31),)
            fine = attend(q0[rows], [k[window] for k in k0], [v[window] for v in v0], masks)
            _, mass, summary = merge(tuple(a[rows] for a in level), fine)
            ab[c, rows] = (summary / mass).astype(BF)
        send(ab.at[c, at(ROWS * (1 - h), ROWS)], ret.at[c], rs.at[c], rr.at[c], partner)

    spread(0)
    coarse_spread()
    spread(1)
    coarse_attend()
    spread(2)
    coarse_received()
    compute(0)
    spread(3)
    compute(1)
    compute(2)
    compute(3)

    w_copy.wait()
    for c in range(CHUNKS):
        part = jnp.dot(
            ab[c, at(ROWS * h, ROWS)], wv[at(HALF * h + LANES * c, LANES)], preferred_element_type=F32
        )
        if c == 0:
            acc[...] = part
        else:
            acc[...] += part
    for c in range(CHUNKS):
        received(ret.at[c], rs.at[c], rr.at[c])
        part = jnp.dot(ret[c], wv[at(HALF * (1 - h) + LANES * c, LANES)], preferred_element_type=F32)
        if c < CHUNKS - 1:
            acc[...] += part
        else:
            out_ref[...] = (acc[...] + part).astype(BF)
    for copy in sent:
        copy.wait_send()


def local(queries, keys, values, out_weight):
    vmem = pltpu.VMEM
    dma = pltpu.SemaphoreType.DMA
    scratch = [
        vmem((3, ROWS, D), BF),
        vmem((CHUNKS, 512, LANES), BF),
        vmem((CHUNKS, 768, LANES), BF),
        vmem((CHUNKS, 768, LANES), BF),
        vmem((D, D), BF),
        vmem((8, 3, 16, LANES), BF),
        vmem((3, 128, LANES), BF),
        vmem((2, 128, LANES), BF),
        vmem((2, 64, LANES), BF),
        vmem((2, 32, LANES), BF),
        vmem((2, 128, LANES), BF),
        vmem((2, 128, LANES), BF),
        vmem((2, 128, LANES), BF),
        vmem((4, 3, 32, LANES), F32),
        vmem((4, 3, 32, LANES), F32),
        vmem((CHUNKS, 2, 128, LANES), BF),
        vmem((CHUNKS, 2, 128, LANES), BF),
        vmem((CHUNKS, 2, 64, LANES), BF),
        vmem((CHUNKS, 2, 128, LANES), BF),
        vmem((CHUNKS, 512, LANES), BF),
        vmem((CHUNKS, ROWS, LANES), BF),
        vmem((ROWS, D), F32),
        vmem((3, 512, LANES), F32),
        dma((3,)),
        dma((CHUNKS, 3)),
        dma,
        dma((CHUNKS, 3)),
        dma((CHUNKS, 3)),
        dma((CHUNKS, 2)),
        dma((CHUNKS, 2)),
        dma((CHUNKS, 2)),
        dma((CHUNKS, 2)),
        dma((CHUNKS,)),
        dma((CHUNKS,)),
        dma((CHUNKS, 2)),
        dma((CHUNKS, 2)),
        dma((8,)),
        dma((8,)),
        dma((7,)),
        dma((7,)),
        dma((4,)),
        dma((4,)),
        dma((CHUNKS,)),
        dma((CHUNKS,)),
        dma,
    ]
    anywhere = pl.BlockSpec(memory_space=pl.ANY)
    return pl.pallas_call(
        kernel,
        out_shape=jax.ShapeDtypeStruct((ROWS, D), BF),
        in_specs=[anywhere] * 4,
        out_specs=pl.BlockSpec(memory_space=pltpu.VMEM),
        scratch_shapes=scratch,
        compiler_params=pltpu.CompilerParams(
            collective_id=0, has_side_effects=True, vmem_limit_bytes=40 << 20
        ),
        cost_estimate=pl.CostEstimate(flops=1 << 30, bytes_accessed=4 << 20, transcendentals=1 << 21),
    )(queries, keys, values, out_weight)


def solution(mesh):
    rows = P(("batch", "seq"), None)
    return jax.shard_map(
        local, mesh=mesh, in_specs=(rows, rows, rows, P()), out_specs=rows, check_vma=False
    )
```

```python
import math

import jax
import jax.numpy as jnp
from jax import lax
from jax.experimental import pallas as pl
from jax.experimental.pallas import tpu as pltpu
from jax.sharding import PartitionSpec as P

MESH = pl.DeviceIdType.MESH
ROWS = 256
BLOCK = 128
D = 1024
HALF = 512
LANES = 128
CHUNKS = 4
FACTOR = math.log2(math.e) / 8.0
BF, F32 = jnp.bfloat16, jnp.float32
MASKED = -1e30


def averaging(rows):
    i = lax.broadcasted_iota(jnp.int32, (rows // 2, rows), 0)
    j = lax.broadcasted_iota(jnp.int32, (rows // 2, rows), 1)
    return jnp.where((j == 2 * i) | (j == 2 * i + 1), 0.5, 0.0).astype(BF)


def coarsen(x):
    rows = x.shape[0]
    if rows > 256:
        return jnp.concatenate([coarsen(x[i : i + 256]) for i in range(0, rows, 256)], axis=0)
    return jnp.dot(averaging(rows), x, preferred_element_type=F32).astype(BF)


def low_lanes(rows):
    return lax.broadcasted_iota(jnp.int32, (rows, LANES), 1) < 64


def split_keys(k):
    low, zero = low_lanes(k.shape[0]), jnp.zeros_like(k)
    return jnp.where(low, k, zero), jnp.where(low, zero, k)


def split_values(v):
    low, zero, one = low_lanes(v.shape[0]), jnp.zeros_like(v), jnp.ones_like(v)
    return (
        jnp.concatenate([jnp.where(low, v, zero), jnp.where(low, one, zero)], axis=1),
        jnp.concatenate([jnp.where(low, zero, v), jnp.where(low, zero, one)], axis=1),
    )


def attend(q, keys, values, masks=()):
    weights, peaks = [], []
    for k in keys:
        s = lax.dot_general(q, k, (((1,), (1,)), ((), ())), preferred_element_type=F32)
        for first, last, hidden in masks:
            parts = [s[:, :first], jnp.where(hidden, MASKED, s[:, first:last]), s[:, last:]]
            s = jnp.concatenate([part for part in parts if part.shape[1]], axis=1)
        peak = jnp.max(s, axis=1, keepdims=True)
        weights.append(jnp.exp2((s - peak) * FACTOR).astype(BF))
        peaks.append(peak * FACTOR)
    total = jnp.dot(
        jnp.concatenate(weights, axis=1), jnp.concatenate(values, axis=0), preferred_element_type=F32
    )
    peak = jnp.where(low_lanes(q.shape[0]), peaks[0], peaks[1])
    return peak, total[:, LANES:], total[:, :LANES]


def merge(a, b):
    peak = jnp.maximum(a[0], b[0])
    scale_a, scale_b = jnp.exp2(a[0] - peak), jnp.exp2(b[0] - peak)
    return peak, scale_a * a[1] + scale_b * b[1], scale_a * a[2] + scale_b * b[2]


def kernel(q_hbm, k_hbm, v_hbm, w_hbm, out_ref, *scratch):
    (own, qp, kx, vx, wv, st4, r4, z4s, z5s, z6s, z4r, z5r, z6r, cos, cor, s2, r2, s3, r3, ab, ret, acc, rep, held, kv1, k0s, v0s,
     own_sem, pair_sem, w_sem, e1s, e1r, nats, natr, rels, relr, s2s, s2r, s3s, s3r, a2as, a2ar, zs, zr, cs, cr,
     rs, rr, self_sem, plane_sem, z_sem) = scratch
    b, s = lax.axis_index("batch"), lax.axis_index("seq")
    h, x, z, p = s % 2, (s // 2) % 4, s // 8, s // 2
    me8 = s % 8
    partner = (b, p * 2 + 1 - h)

    def pair(index):
        return (b, index * 2 + h)

    def in_plane(x2):
        return (b, z * 8 + x2 * 2 + h)

    def along_z(z2):
        return (b, z2 * 8 + me8)

    def flip(v, bits):
        for bit in (1, 2, 4):
            if bits & bit:
                v = v + bit - 2 * bit * ((v // bit) % 2)
        return v

    def remote(src, dst, ssem, rsem, target):
        return pltpu.make_async_remote_copy(
            src_ref=src, dst_ref=dst, send_sem=ssem, recv_sem=rsem, device_id=target, device_id_type=MESH
        )

    sent = []

    def send(*args):
        copy = remote(*args)
        copy.start()
        sent.append(copy)

    def received(dst, ssem, rsem):
        remote(dst, dst, ssem, rsem, partner).wait_recv()

    def signal(sem, target):
        pl.semaphore_signal(sem, inc=1, device_id=target, device_id_type=MESH)

    def signal_z(sem, far):
        @pl.when(z >= far)
        def _():
            signal(sem, along_z(z - far))

        @pl.when(z < 8 - far)
        def _():
            signal(sem, along_z(z + far))

    def count_z(far):
        return jnp.where(z >= far, 1, 0) + jnp.where(z < 8 - far, 1, 0)

    barrier = pltpu.get_barrier_semaphore()
    signal(barrier, partner)
    for j in range(1, 4):
        signal(barrier, in_plane((x + j) % 4))
    signal_z(barrier, 1)

    inputs = (q_hbm, k_hbm, v_hbm)
    own_copies = [pltpu.make_async_copy(inputs[i], own.at[i], own_sem.at[i]) for i in range(3)]
    for copy in own_copies:
        copy.start()

    def mine(c):
        return pl.ds(pl.multiple_of(h * HALF + c * LANES, LANES), LANES)

    def theirs(c):
        return pl.ds(pl.multiple_of((1 - h) * HALF + c * LANES, LANES), LANES)

    def at(start, size):
        return pl.ds(pl.multiple_of(start, 128), size)

    pair_refs = (qp, kx, vx)
    offsets = (0, BLOCK, BLOCK)
    pair_copies = []
    for c in range(CHUNKS):
        for i in range(3):
            copy = pltpu.make_async_copy(
                inputs[i].at[:, mine(c)], pair_refs[i].at[c, at(offsets[i] + ROWS * h, ROWS)], pair_sem.at[c, i]
            )
            copy.start()
            pair_copies.append(copy)
    w_copy = pltpu.make_async_copy(w_hbm, wv, w_sem)
    w_copy.start()

    def exchange(c, i):
        send(
            inputs[i].at[:, theirs(c)],
            pair_refs[i].at[c, at(offsets[i] + ROWS * h, ROWS)],
            e1s.at[c, i],
            e1r.at[c, i],
            partner,
        )

    def exchanged(c, i):
        received(pair_refs[i].at[c, at(offsets[i] + ROWS * (1 - h), ROWS)], e1s.at[c, i], e1r.at[c, i])

    def level4():
        for i in range(3):
            own_copies[i].wait()
        coarse = [own[i] for i in range(3)]
        for _ in range(4):
            coarse = [coarsen(level) for level in coarse]
        for i in range(3):
            for hp in range(8):
                st4[(hp % 4) * 2 + hp // 4, i] = coarse[i][:, hp * LANES : (hp + 1) * LANES]
        pl.semaphore_wait(plane_sem, 1)
        for j in range(1, 8):
            t = (me8 + j) % 8
            send(
                st4.at[t], r4.at[:, pl.ds(pl.multiple_of(me8 * 16, 16), 16)], a2as.at[t], a2ar.at[me8], (b, z * 8 + t)
            )
        self_copy.start()

    self_copy = pltpu.make_async_copy(st4.at[me8], r4.at[:, pl.ds(pl.multiple_of(me8 * 16, 16), 16)], self_sem)

    native_pair, relay_pair = p - 1 + 2 * h, p + 1 - 2 * h
    native_there = (native_pair >= 0) & (native_pair <= 31)
    relay_there = (relay_pair >= 0) & (relay_pair <= 31)

    def native_rim(c, i):
        return remote(
            inputs[i].at[at(BLOCK * h, BLOCK), mine(c)],
            pair_refs[i].at[c, at(640 * (1 - h), BLOCK)],
            nats.at[c, i - 1],
            natr.at[c, i - 1],
            pair(native_pair),
        )

    def relay_rim(c, i):
        return remote(
            pair_refs[i].at[c, at(BLOCK * (4 - 3 * h), BLOCK)],
            pair_refs[i].at[c, at(640 * h, BLOCK)],
            rels.at[c, i - 1],
            relr.at[c, i - 1],
            pair(relay_pair),
        )

    def native_rims():
        @pl.when(native_there)
        def _():
            for c in range(CHUNKS):
                for i in (1, 2):
                    native_rim(c, i).start()

    def rims_received(c):
        @pl.when(relay_there)
        def _():
            for i in (1, 2):
                received(pair_refs[i].at[c, at(640 * (1 - h), BLOCK)], nats.at[c, i - 1], natr.at[c, i - 1])

        @pl.when(native_there)
        def _():
            for i in (1, 2):
                received(pair_refs[i].at[c, at(640 * h, BLOCK)], rels.at[c, i - 1], relr.at[c, i - 1])

    def rims_sent():
        @pl.when(native_there)
        def _():
            for c in range(CHUNKS):
                for i in (1, 2):
                    native_rim(c, i).wait_send()

        @pl.when(relay_there)
        def _():
            for c in range(CHUNKS):
                for i in (1, 2):
                    relay_rim(c, i).wait_send()

    def no_rims():
        @pl.when(p == 0)
        def _():
            for ref in (kx, vx):
                ref[:, :BLOCK] = jnp.zeros((CHUNKS, BLOCK, LANES), BF)

        @pl.when(p == 31)
        def _():
            for ref in (kx, vx):
                ref[:, 640:] = jnp.zeros((CHUNKS, BLOCK, LANES), BF)

    def spread(c):
        for i in (1, 2):
            pair_copies[c * 3 + i].wait()
            exchanged(c, i)

        @pl.when(relay_there)
        def _():
            for i in (1, 2):
                relay_rim(c, i).start()

        fine = jnp.concatenate([kx[c, BLOCK : BLOCK + 512], vx[c, BLOCK : BLOCK + 512]], axis=1)
        level1 = coarsen(fine)
        level2 = coarsen(level1)
        level3 = coarsen(level2)
        for i in range(2):
            side = slice(LANES * i, LANES * i + LANES)
            s2[c, i] = level2[:, side]
            s3[c, i] = level3[:, side]
            kv1[c, i] = level1[:, side]
        send(s2.at[c], r2.at[c], s2s.at[c], s2r.at[c], in_plane(flip(x, 1)))
        for k in (0, 1):
            send(
                s3.at[c], r3.at[c, :, pl.ds(64 * k, 64)], s3s.at[c, k], s3r.at[c, k], in_plane(flip(x, 2 + k))
            )

    def coarse_spread():
        self_copy.wait()
        for j in range(1, 8):
            t = (me8 + j) % 8
            received(r4.at[:, pl.ds(pl.multiple_of(t * 16, 16), 16)], a2as.at[t], a2ar.at[t])
        for i in (1, 2):
            level4 = r4[i]
            level5 = coarsen(level4)
            z4s[i - 1] = level4
            z5s[i - 1] = level5
            z6s[i - 1] = coarsen(level5)
        pl.semaphore_wait(z_sem.at[2], count_z(4))
        send(z4s, z4r, zs.at[0], zr.at[0], along_z(flip(z, 1)))
        for k in range(2):
            send(z5s, z5r.at[:, pl.ds(64 * k, 64)], zs.at[1 + k], zr.at[1 + k], along_z(flip(z, 2 + k)))
        for k in range(4):
            send(z6s, z6r.at[:, pl.ds(32 * k, 32)], zs.at[3 + k], zr.at[3 + k], along_z(flip(z, 4 + k)))

    def repeated(level):
        rows = level[0].shape[0]
        for i in range(3):
            rep[i, pl.ds(0, rows, stride=2), :] = level[i]
            rep[i, pl.ds(1, rows, stride=2), :] = level[i]
        return tuple(rep[i, : 2 * rows, :] for i in range(3))

    def coarse_attend():
        received(z4r, zs.at[0], zr.at[0])
        for k in range(2):
            received(z5r.at[:, pl.ds(64 * k, 64)], zs.at[1 + k], zr.at[1 + k])
        for k in range(4):
            received(z6r.at[:, pl.ds(32 * k, 32)], zs.at[3 + k], zr.at[3 + k])
        q4 = r4[0]
        q5 = coarsen(q4)
        q6 = coarsen(q5)
        level = attend(q6, split_keys(z6r[0]), split_values(z6r[1]))
        level = merge(repeated(level), attend(q5, split_keys(z5r[0]), split_values(z5r[1])))
        level = merge(repeated(level), attend(q4, split_keys(z4r[0]), split_values(z4r[1])))
        for i in range(3):
            for x2 in range(4):
                cos[x2, i] = level[i][x2 * 32 : x2 * 32 + 32]
        for j in range(1, 4):
            x2 = (x + j) % 4
            send(cos.at[x2], cor.at[x], cs.at[x2], cr.at[x], in_plane(x2))
        local = pltpu.make_async_copy(cos.at[x], cor.at[x], self_sem)
        local.start()
        local.wait()

    def coarse_received():
        for j in range(1, 4):
            x2 = (x + j) % 4
            received(cor.at[x2], cs.at[x2], cr.at[x2])

    def windows(c, deferred):
        pair_copies[c * 3].wait()
        exchanged(c, 0)
        rims_received(c)
        received(r2.at[c], s2s.at[c], s2r.at[c])
        for k in (0, 1):
            received(r3.at[c, :, pl.ds(64 * k, 64)], s3s.at[c, k], s3r.at[c, k])
        q0 = qp[c]
        q1 = coarsen(q0)
        q2 = coarsen(q1)
        q3 = coarsen(q2)
        level = attend(q3, split_keys(r3[c, 0]), split_values(r3[c, 1]))
        if not deferred:
            level = merge(repeated(tuple(cor[c, i] for i in range(3))), level)
        level = merge(repeated(level), attend(q2, split_keys(r2[c, 0]), split_values(r2[c, 1])))
        k1 = split_keys(kv1[c, 0])
        v1 = split_values(kv1[c, 1])
        parts = []
        for block in (0, 1):
            other = slice(128 * (1 - block), 128 * (2 - block))
            parts.append(attend(q1[128 * block : 128 * block + 128], [k[other] for k in k1], [v[other] for v in v1]))
        fine = tuple(jnp.concatenate([part[i] for part in parts], axis=0) for i in range(3))
        level = repeated(merge(repeated(level), fine))
        for head, (k0, v0) in enumerate(zip(split_keys(kx[c]), split_values(vx[c]))):
            k0s[head] = k0
            v0s[head] = v0
        for block in range(4):
            window = slice(128 * block, 128 * block + 384)
            rows = slice(128 * block, 128 * block + 128)
            masks = ()
            if block == 0:
                masks = ((0, 128, p == 0),)
            if block == 3:
                masks = ((256, 384, p == 31),)
            fine = attend(q0[rows], [k0s[0, window], k0s[1, window]], [v0s[0, window], v0s[1, window]], masks)
            merged = merge(tuple(a[rows] for a in level), fine)
            if deferred:
                for i in range(3):
                    held[c, i, rows] = merged[i]
            else:
                ab[c, rows] = (merged[2] / merged[1]).astype(BF)

    def late_merge(c):
        for i in range(3):
            level = cor[c, i]
            for k in range(16):
                rep[i, pl.ds(k, 32, stride=16), :] = level
        for block in range(4):
            rows = slice(128 * block, 128 * block + 128)
            _, mass, summary = merge(tuple(rep[i, rows] for i in range(3)), tuple(held[c, i, rows] for i in range(3)))
            ab[c, rows] = (summary / mass).astype(BF)

    def give_back(c):
        send(ab.at[c, at(ROWS * (1 - h), ROWS)], ret.at[c], rs.at[c], rr.at[c], partner)

    no_rims()
    pl.semaphore_wait(barrier, 4 + count_z(1))
    signal(plane_sem, partner)
    signal_z(z_sem.at[0], 1)
    exchange(0, 1)
    exchange(0, 2)
    level4()
    for c, i in ((1, 1), (1, 2), (0, 0), (2, 1), (2, 2), (1, 0), (3, 1), (3, 2), (2, 0), (3, 0)):
        exchange(c, i)
    pl.semaphore_wait(z_sem.at[0], count_z(1))
    signal_z(z_sem.at[1], 2)
    native_rims()
    spread(0)
    pl.semaphore_wait(z_sem.at[1], count_z(2))
    signal_z(z_sem.at[2], 4)
    spread(1)
    coarse_spread()
    windows(0, True)
    spread(2)
    windows(1, True)
    coarse_attend()
    spread(3)
    windows(2, True)
    coarse_received()
    late_merge(0)
    give_back(0)
    late_merge(1)
    give_back(1)
    late_merge(2)
    give_back(2)
    windows(3, False)
    give_back(3)

    w_copy.wait()
    for c in range(CHUNKS):
        part = jnp.dot(
            ab[c, at(ROWS * h, ROWS)], wv[at(HALF * h + LANES * c, LANES)], preferred_element_type=F32
        )
        if c == 0:
            acc[...] = part
        else:
            acc[...] += part
    for c in range(CHUNKS):
        received(ret.at[c], rs.at[c], rr.at[c])
        part = jnp.dot(ret[c], wv[at(HALF * (1 - h) + LANES * c, LANES)], preferred_element_type=F32)
        if c < CHUNKS - 1:
            acc[...] += part
        else:
            out_ref[...] = (acc[...] + part).astype(BF)
    for copy in sent:
        copy.wait_send()
    rims_sent()


def local(queries, keys, values, out_weight):
    vmem = pltpu.VMEM
    dma = pltpu.SemaphoreType.DMA
    scratch = [
        vmem((3, ROWS, D), BF),
        vmem((CHUNKS, 512, LANES), BF),
        vmem((CHUNKS, 768, LANES), BF),
        vmem((CHUNKS, 768, LANES), BF),
        vmem((D, D), BF),
        vmem((8, 3, 16, LANES), BF),
        vmem((3, 128, LANES), BF),
        vmem((2, 128, LANES), BF),
        vmem((2, 64, LANES), BF),
        vmem((2, 32, LANES), BF),
        vmem((2, 128, LANES), BF),
        vmem((2, 128, LANES), BF),
        vmem((2, 128, LANES), BF),
        vmem((4, 3, 32, LANES), F32),
        vmem((4, 3, 32, LANES), F32),
        vmem((CHUNKS, 2, 128, LANES), BF),
        vmem((CHUNKS, 2, 128, LANES), BF),
        vmem((CHUNKS, 2, 64, LANES), BF),
        vmem((CHUNKS, 2, 128, LANES), BF),
        vmem((CHUNKS, 512, LANES), BF),
        vmem((CHUNKS, ROWS, LANES), BF),
        vmem((ROWS, D), F32),
        vmem((3, 512, LANES), F32),
        vmem((CHUNKS, 3, 512, LANES), F32),
        vmem((CHUNKS, 2, 256, LANES), BF),
        vmem((2, 768, LANES), BF),
        vmem((2, 768, 2 * LANES), BF),
        dma((3,)),
        dma((CHUNKS, 3)),
        dma,
        dma((CHUNKS, 3)),
        dma((CHUNKS, 3)),
        dma((CHUNKS, 2)),
        dma((CHUNKS, 2)),
        dma((CHUNKS, 2)),
        dma((CHUNKS, 2)),
        dma((CHUNKS,)),
        dma((CHUNKS,)),
        dma((CHUNKS, 2)),
        dma((CHUNKS, 2)),
        dma((8,)),
        dma((8,)),
        dma((7,)),
        dma((7,)),
        dma((4,)),
        dma((4,)),
        dma((CHUNKS,)),
        dma((CHUNKS,)),
        dma,
        pltpu.SemaphoreType.REGULAR,
        pltpu.SemaphoreType.REGULAR((3,)),
    ]
    anywhere = pl.BlockSpec(memory_space=pl.ANY)
    return pl.pallas_call(
        kernel,
        out_shape=jax.ShapeDtypeStruct((ROWS, D), BF),
        in_specs=[anywhere] * 4,
        out_specs=pl.BlockSpec(memory_space=pltpu.VMEM),
        scratch_shapes=scratch,
        compiler_params=pltpu.CompilerParams(
            collective_id=0, has_side_effects=True, vmem_limit_bytes=56 << 20
        ),
        cost_estimate=pl.CostEstimate(flops=1 << 30, bytes_accessed=4 << 20, transcendentals=1 << 21),
    )(queries, keys, values, out_weight)


def solution(mesh):
    rows = P(("batch", "seq"), None)
    return jax.shard_map(
        local, mesh=mesh, in_specs=(rows, rows, rows, P()), out_specs=rows, check_vma=False
    )
```

```python
import math

import jax
import jax.numpy as jnp
from jax import lax
from jax.experimental import pallas as pl
from jax.experimental.pallas import tpu as pltpu
from jax.sharding import PartitionSpec as P

MESH = pl.DeviceIdType.MESH
ROWS = 256
BLOCK = 128
D = 1024
HALF = 512
LANES = 128
CHUNKS = 4
FACTOR = math.log2(math.e) / 8.0
BF, F32 = jnp.bfloat16, jnp.float32
MASKED = -1e30


def averaging(rows):
    i = lax.broadcasted_iota(jnp.int32, (rows // 2, rows), 0)
    j = lax.broadcasted_iota(jnp.int32, (rows // 2, rows), 1)
    return jnp.where((j == 2 * i) | (j == 2 * i + 1), 0.5, 0.0).astype(BF)


def coarsen(x):
    rows = x.shape[0]
    if rows > 256:
        return jnp.concatenate([coarsen(x[i : i + 256]) for i in range(0, rows, 256)], axis=0)
    return jnp.dot(averaging(rows), x, preferred_element_type=F32).astype(BF)


def low_lanes(rows):
    return lax.broadcasted_iota(jnp.int32, (rows, LANES), 1) < 64


def split_keys(k):
    low, zero = low_lanes(k.shape[0]), jnp.zeros_like(k)
    return jnp.where(low, k, zero), jnp.where(low, zero, k)


def split_values(v):
    low, zero, one = low_lanes(v.shape[0]), jnp.zeros_like(v), jnp.ones_like(v)
    return (
        jnp.concatenate([jnp.where(low, v, zero), jnp.where(low, one, zero)], axis=1),
        jnp.concatenate([jnp.where(low, zero, v), jnp.where(low, zero, one)], axis=1),
    )


def scored(q, keys, values, hidden=None):
    scores = []
    for k in keys():
        s = lax.dot_general(q(), k, (((1,), (1,)), ((), ())), preferred_element_type=F32)
        if hidden is not None:
            first, last, masked = hidden
            parts = [s[:, :first], jnp.where(masked, MASKED, s[:, first:last]), s[:, last:]]
            s = jnp.concatenate([part for part in parts if part.shape[1]], axis=1)
        scores.append(s)
    return scores


def weighted(scores):
    weights, peaks = [], []
    for s in scores:
        peak = jnp.max(s, axis=1, keepdims=True)
        weights.append(jnp.exp2((s - peak) * FACTOR).astype(BF))
        peaks.append(peak * FACTOR)
    return jnp.concatenate(weights, axis=1), jnp.where(low_lanes(scores[0].shape[0]), peaks[0], peaks[1])


def summed(weights, peak, values):
    total = jnp.dot(weights, jnp.concatenate(values, axis=0), preferred_element_type=F32)
    return peak, total[:, LANES:], total[:, :LANES]


def attend(units, done=None):
    scores, weights, results = {}, {}, []
    for step in range(len(units) + 3):
        if step < len(units):
            scores[step] = scored(*units[step])
        if 0 <= step - 2 < len(units):
            weights[step - 2] = weighted(scores.pop(step - 2))
        if step >= 3:
            result = summed(*weights.pop(step - 3), units[step - 3][2]())
            results.append(result if done is None else done(step - 3, result))
    return results


def merge(a, b):
    peak = jnp.maximum(a[0], b[0])
    scale_a, scale_b = jnp.exp2(a[0] - peak), jnp.exp2(b[0] - peak)
    return peak, scale_a * a[1] + scale_b * b[1], scale_a * a[2] + scale_b * b[2]


def kernel(q_hbm, k_hbm, v_hbm, w_hbm, out_ref, *scratch):
    (own, qp, kx, vx, wv, st4, r4, z4s, z5s, z6s, z4r, z5r, z6r, cos, cor, s2, r2, s3, r3, ab, ret, acc, rep, held, kv1, k0s, v0s,
     own_sem, pair_sem, w_sem, e1s, e1r, nats, natr, rels, relr, s2s, s2r, s3s, s3r, a2as, a2ar, zs, zr, cs, cr,
     rs, rr, self_sem, plane_sem, z_sem) = scratch
    b, s = lax.axis_index("batch"), lax.axis_index("seq")
    h, x, z, p = s % 2, (s // 2) % 4, s // 8, s // 2
    me8 = s % 8
    partner = (b, p * 2 + 1 - h)

    def pair(index):
        return (b, index * 2 + h)

    def in_plane(x2):
        return (b, z * 8 + x2 * 2 + h)

    def along_z(z2):
        return (b, z2 * 8 + me8)

    def flip(v, bits):
        for bit in (1, 2, 4):
            if bits & bit:
                v = v + bit - 2 * bit * ((v // bit) % 2)
        return v

    def remote(src, dst, ssem, rsem, target):
        return pltpu.make_async_remote_copy(
            src_ref=src, dst_ref=dst, send_sem=ssem, recv_sem=rsem, device_id=target, device_id_type=MESH
        )

    sent = []

    def send(*args):
        copy = remote(*args)
        copy.start()
        sent.append(copy)

    def received(dst, ssem, rsem):
        remote(dst, dst, ssem, rsem, partner).wait_recv()

    def signal(sem, target):
        pl.semaphore_signal(sem, inc=1, device_id=target, device_id_type=MESH)

    def signal_z(sem, far):
        @pl.when(z >= far)
        def _():
            signal(sem, along_z(z - far))

        @pl.when(z < 8 - far)
        def _():
            signal(sem, along_z(z + far))

    def count_z(far):
        return jnp.where(z >= far, 1, 0) + jnp.where(z < 8 - far, 1, 0)

    barrier = pltpu.get_barrier_semaphore()
    signal(barrier, partner)
    for j in range(1, 4):
        signal(barrier, in_plane((x + j) % 4))
    signal_z(barrier, 1)

    inputs = (q_hbm, k_hbm, v_hbm)
    own_copies = [pltpu.make_async_copy(inputs[i], own.at[i], own_sem.at[i]) for i in range(3)]
    for copy in own_copies:
        copy.start()

    def mine(c):
        return pl.ds(pl.multiple_of(h * HALF + c * LANES, LANES), LANES)

    def theirs(c):
        return pl.ds(pl.multiple_of((1 - h) * HALF + c * LANES, LANES), LANES)

    def at(start, size):
        return pl.ds(pl.multiple_of(start, 128), size)

    pair_refs = (qp, kx, vx)
    offsets = (0, BLOCK, BLOCK)
    pair_copies = []
    for c in range(CHUNKS):
        for i in range(3):
            copy = pltpu.make_async_copy(
                inputs[i].at[:, mine(c)], pair_refs[i].at[c, at(offsets[i] + ROWS * h, ROWS)], pair_sem.at[c, i]
            )
            copy.start()
            pair_copies.append(copy)
    w_copy = pltpu.make_async_copy(w_hbm, wv, w_sem)
    w_copy.start()

    def exchange(c, i):
        send(
            inputs[i].at[:, theirs(c)],
            pair_refs[i].at[c, at(offsets[i] + ROWS * h, ROWS)],
            e1s.at[c, i],
            e1r.at[c, i],
            partner,
        )

    def exchanged(c, i):
        received(pair_refs[i].at[c, at(offsets[i] + ROWS * (1 - h), ROWS)], e1s.at[c, i], e1r.at[c, i])

    def level4():
        for i in range(3):
            own_copies[i].wait()
        coarse = [own[i] for i in range(3)]
        for _ in range(4):
            coarse = [coarsen(level) for level in coarse]
        for i in range(3):
            for hp in range(8):
                st4[(hp % 4) * 2 + hp // 4, i] = coarse[i][:, hp * LANES : (hp + 1) * LANES]

    def level4_spread():
        pl.semaphore_wait(plane_sem, 1)
        for j in range(1, 8):
            t = (me8 + j) % 8
            send(
                st4.at[t], r4.at[:, pl.ds(pl.multiple_of(me8 * 16, 16), 16)], a2as.at[t], a2ar.at[me8], (b, z * 8 + t)
            )
        self_copy.start()

    self_copy = pltpu.make_async_copy(st4.at[me8], r4.at[:, pl.ds(pl.multiple_of(me8 * 16, 16), 16)], self_sem)

    native_pair, relay_pair = p - 1 + 2 * h, p + 1 - 2 * h
    native_there = (native_pair >= 0) & (native_pair <= 31)
    relay_there = (relay_pair >= 0) & (relay_pair <= 31)

    def native_rim(c, i):
        return remote(
            inputs[i].at[at(BLOCK * h, BLOCK), mine(c)],
            pair_refs[i].at[c, at(640 * (1 - h), BLOCK)],
            nats.at[c, i - 1],
            natr.at[c, i - 1],
            pair(native_pair),
        )

    def relay_rim(c, i):
        return remote(
            pair_refs[i].at[c, at(BLOCK * (4 - 3 * h), BLOCK)],
            pair_refs[i].at[c, at(640 * h, BLOCK)],
            rels.at[c, i - 1],
            relr.at[c, i - 1],
            pair(relay_pair),
        )

    def native_rims(c):
        @pl.when(native_there)
        def _():
            for i in (1, 2):
                native_rim(c, i).start()

    def rims_received(c):
        @pl.when(relay_there)
        def _():
            for i in (1, 2):
                received(pair_refs[i].at[c, at(640 * (1 - h), BLOCK)], nats.at[c, i - 1], natr.at[c, i - 1])

        @pl.when(native_there)
        def _():
            for i in (1, 2):
                received(pair_refs[i].at[c, at(640 * h, BLOCK)], rels.at[c, i - 1], relr.at[c, i - 1])

    def rims_sent():
        @pl.when(native_there)
        def _():
            for c in range(CHUNKS):
                for i in (1, 2):
                    native_rim(c, i).wait_send()

        @pl.when(relay_there)
        def _():
            for c in range(CHUNKS):
                for i in (1, 2):
                    relay_rim(c, i).wait_send()

    def no_rims():
        @pl.when(p == 0)
        def _():
            for ref in (kx, vx):
                ref[:, :BLOCK] = jnp.zeros((CHUNKS, BLOCK, LANES), BF)

        @pl.when(p == 31)
        def _():
            for ref in (kx, vx):
                ref[:, 640:] = jnp.zeros((CHUNKS, BLOCK, LANES), BF)

    def spread(c):
        for i in (1, 2):
            pair_copies[c * 3 + i].wait()
            exchanged(c, i)

        @pl.when(relay_there)
        def _():
            for i in (1, 2):
                relay_rim(c, i).start()

        fine = jnp.concatenate([kx[c, BLOCK : BLOCK + 512], vx[c, BLOCK : BLOCK + 512]], axis=1)
        level1 = coarsen(fine)
        level2 = coarsen(level1)
        level3 = coarsen(level2)
        for i in range(2):
            side = slice(LANES * i, LANES * i + LANES)
            s2[c, i] = level2[:, side]
            s3[c, i] = level3[:, side]
            kv1[c, i] = level1[:, side]
        send(s2.at[c], r2.at[c], s2s.at[c], s2r.at[c], in_plane(flip(x, 1)))
        for k in (0, 1):
            send(
                s3.at[c], r3.at[c, :, pl.ds(64 * k, 64)], s3s.at[c, k], s3r.at[c, k], in_plane(flip(x, 2 + k))
            )

    def coarse_spread():
        self_copy.wait()
        for j in range(1, 8):
            t = (me8 + j) % 8
            received(r4.at[:, pl.ds(pl.multiple_of(t * 16, 16), 16)], a2as.at[t], a2ar.at[t])
        for i in (1, 2):
            level4 = r4[i]
            level5 = coarsen(level4)
            z4s[i - 1] = level4
            z5s[i - 1] = level5
            z6s[i - 1] = coarsen(level5)
        send(z4s, z4r, zs.at[0], zr.at[0], along_z(flip(z, 1)))
        for k in range(2):
            send(z5s, z5r.at[:, pl.ds(64 * k, 64)], zs.at[1 + k], zr.at[1 + k], along_z(flip(z, 2 + k)))

    def far_copies():
        return [
            remote(z6s, z6r.at[:, pl.ds(32 * k, 32)], zs.at[3 + k], zr.at[3 + k], along_z(flip(z, 4 + k)))
            for k in range(4)
        ]

    def coarse_far():
        pl.semaphore_wait(z_sem.at[2], 1)
        for copy in far_copies():
            copy.start()

    def coarse_far_late_planes():
        pl.when(z >= 4)(coarse_far)

    def coarse_far_early_planes():
        pl.when(z < 4)(coarse_far)

    def repeated(level):
        rows = level[0].shape[0]
        for i in range(3):
            rep[i, pl.ds(0, rows, stride=2), :] = level[i]
            rep[i, pl.ds(1, rows, stride=2), :] = level[i]
        return tuple(rep[i, : 2 * rows, :] for i in range(3))

    def coarse_attend():
        received(z4r, zs.at[0], zr.at[0])
        for k in range(2):
            received(z5r.at[:, pl.ds(64 * k, 64)], zs.at[1 + k], zr.at[1 + k])
        for k in range(4):
            received(z6r.at[:, pl.ds(32 * k, 32)], zs.at[3 + k], zr.at[3 + k])
        q4 = r4[0]
        q5 = coarsen(q4)
        q6 = coarsen(q5)
        level, level5, level4 = attend([
            (lambda q=q, r=r: q, lambda r=r: split_keys(r[0]), lambda r=r: split_values(r[1]))
            for q, r in ((q6, z6r), (q5, z5r), (q4, z4r))
        ])
        level = merge(repeated(level), level5)
        level = merge(repeated(level), level4)
        for i in range(3):
            for x2 in range(4):
                cos[x2, i] = level[i][x2 * 32 : x2 * 32 + 32]
        for j in range(1, 4):
            x2 = (x + j) % 4
            send(cos.at[x2], cor.at[x], cs.at[x2], cr.at[x], in_plane(x2))
        local = pltpu.make_async_copy(cos.at[x], cor.at[x], self_sem)
        local.start()
        local.wait()

    def coarse_received():
        for j in range(1, 4):
            x2 = (x + j) % 4
            received(cor.at[x2], cs.at[x2], cr.at[x2])

    def give_back(c):
        send(ab.at[c, at(ROWS * (1 - h), ROWS)], ret.at[c], rs.at[c], rr.at[c], partner)

    def windows(c, deferred):
        pair_copies[c * 3].wait()
        exchanged(c, 0)
        rims_received(c)
        received(r2.at[c], s2s.at[c], s2r.at[c])
        for k in (0, 1):
            received(r3.at[c, :, pl.ds(64 * k, 64)], s3s.at[c, k], s3r.at[c, k])
        q0 = qp[c]
        q1 = coarsen(q0)
        q2 = coarsen(q1)
        q3 = coarsen(q2)
        for head, (k0, v0) in enumerate(zip(split_keys(kx[c]), split_values(vx[c]))):
            k0s[head] = k0
            v0s[head] = v0
        k1 = split_keys(kv1[c, 0])
        v1 = split_values(kv1[c, 1])

        def block_of(unit):
            return (2 * (1 - h), 2 * (1 - h) + 1, 2 * h, 2 * h + 1)[unit]

        def fine_unit(unit):
            block = block_of(unit)
            start = BLOCK * block
            hidden = ((0, 128, (p == 0) & (block == 0)), (256, 384, (p == 31) & (block == 3)))[unit % 2]
            return (
                lambda: qp[c, at(start, BLOCK)],
                lambda: [k0s[0, at(start, 384)], k0s[1, at(start, 384)]],
                lambda: [v0s[0, at(start, 384)], v0s[1, at(start, 384)]],
                hidden,
            )

        def sibling_unit(block):
            other = slice(128 * (1 - block), 128 * (2 - block))
            return (
                lambda: q1[128 * block : 128 * block + 128],
                lambda: [k[other] for k in k1],
                lambda: [v[other] for v in v1],
            )

        units = [
            (lambda: q3, lambda: split_keys(r3[c, 0]), lambda: split_values(r3[c, 1])),
            (lambda: q2, lambda: split_keys(r2[c, 0]), lambda: split_values(r2[c, 1])),
            sibling_unit(0),
            sibling_unit(1),
        ] + [fine_unit(unit) for unit in range(4)]
        state = {}

        def done(index, result):
            if index == 0:
                if not deferred:
                    result = merge(repeated(tuple(cor[c, i] for i in range(3))), result)
                state["level"] = result
            elif index == 1:
                state["level"] = merge(repeated(state["level"]), result)
            elif index == 2:
                state["half"] = result
            elif index == 3:
                both = tuple(jnp.concatenate([state["half"][i], result[i]], axis=0) for i in range(3))
                repeated(merge(repeated(state["level"]), both))
            else:
                rows = at(BLOCK * block_of(index - 4), BLOCK)
                merged = merge(tuple(rep[i, rows] for i in range(3)), result)
                if deferred:
                    for i in range(3):
                        held[c, i, rows] = merged[i]
                else:
                    ab[c, rows] = (merged[2] / merged[1]).astype(BF)
                    if index == 5:
                        give_back(c)

        attend(units, done)

    def late_merge(c):
        for i in range(3):
            level = cor[c, i]
            for k in range(16):
                rep[i, pl.ds(k, 32, stride=16), :] = level
        for block in range(4):
            rows = slice(128 * block, 128 * block + 128)
            _, mass, summary = merge(tuple(rep[i, rows] for i in range(3)), tuple(held[c, i, rows] for i in range(3)))
            ab[c, rows] = (summary / mass).astype(BF)

    no_rims()
    level4()
    pl.semaphore_wait(barrier, 4 + count_z(1))
    signal(plane_sem, partner)
    signal_z(z_sem.at[0], 1)
    exchange(0, 1)
    exchange(0, 2)
    level4_spread()
    for c, i in ((1, 1), (1, 2), (0, 0), (2, 1), (2, 2), (3, 1), (3, 2), (1, 0), (2, 0), (3, 0)):
        exchange(c, i)
    pl.semaphore_wait(z_sem.at[0], count_z(1))
    signal_z(z_sem.at[1], 2)
    native_rims(0)
    spread(0)
    native_rims(1)
    pl.semaphore_wait(z_sem.at[1], count_z(2))
    signal_z(z_sem.at[2], 4)
    coarse_spread()
    coarse_far_late_planes()
    spread(1)
    native_rims(2)
    windows(0, True)
    coarse_far_early_planes()
    spread(2)
    coarse_attend()
    native_rims(3)
    spread(3)
    windows(1, True)
    windows(2, True)
    coarse_received()
    late_merge(0)
    give_back(0)
    late_merge(1)
    give_back(1)
    late_merge(2)
    give_back(2)
    windows(3, False)

    def finish():
        for copy in sent + far_copies():
            copy.wait_send()
        rims_sent()

    w_copy.wait()
    for c in range(CHUNKS):
        part = jnp.dot(
            ab[c, at(ROWS * h, ROWS)], wv[at(HALF * h + LANES * c, LANES)], preferred_element_type=F32
        )
        if c == 0:
            acc[...] = part
        else:
            acc[...] += part
    for c in range(CHUNKS):
        received(ret.at[c], rs.at[c], rr.at[c])
        weight = wv[at(HALF * (1 - h) + LANES * c, LANES)]
        if c < CHUNKS - 1:
            acc[...] += jnp.dot(ret[c], weight, preferred_element_type=F32)
        else:
            for i in range(4):
                rows = slice(64 * i, 64 * i + 64)
                part = jnp.dot(ret[c, rows], weight, preferred_element_type=F32)
                out_ref[rows] = (acc[rows] + part).astype(BF)
    finish()


def local(queries, keys, values, out_weight):
    vmem = pltpu.VMEM
    dma = pltpu.SemaphoreType.DMA
    scratch = [
        vmem((3, ROWS, D), BF),
        vmem((CHUNKS, 512, LANES), BF),
        vmem((CHUNKS, 768, LANES), BF),
        vmem((CHUNKS, 768, LANES), BF),
        vmem((D, D), BF),
        vmem((8, 3, 16, LANES), BF),
        vmem((3, 128, LANES), BF),
        vmem((2, 128, LANES), BF),
        vmem((2, 64, LANES), BF),
        vmem((2, 32, LANES), BF),
        vmem((2, 128, LANES), BF),
        vmem((2, 128, LANES), BF),
        vmem((2, 128, LANES), BF),
        vmem((4, 3, 32, LANES), F32),
        vmem((4, 3, 32, LANES), F32),
        vmem((CHUNKS, 2, 128, LANES), BF),
        vmem((CHUNKS, 2, 128, LANES), BF),
        vmem((CHUNKS, 2, 64, LANES), BF),
        vmem((CHUNKS, 2, 128, LANES), BF),
        vmem((CHUNKS, 512, LANES), BF),
        vmem((CHUNKS, ROWS, LANES), BF),
        vmem((ROWS, D), F32),
        vmem((3, 512, LANES), F32),
        vmem((CHUNKS, 3, 512, LANES), F32),
        vmem((CHUNKS, 2, 256, LANES), BF),
        vmem((2, 768, LANES), BF),
        vmem((2, 768, 2 * LANES), BF),
        dma((3,)),
        dma((CHUNKS, 3)),
        dma,
        dma((CHUNKS, 3)),
        dma((CHUNKS, 3)),
        dma((CHUNKS, 2)),
        dma((CHUNKS, 2)),
        dma((CHUNKS, 2)),
        dma((CHUNKS, 2)),
        dma((CHUNKS,)),
        dma((CHUNKS,)),
        dma((CHUNKS, 2)),
        dma((CHUNKS, 2)),
        dma((8,)),
        dma((8,)),
        dma((7,)),
        dma((7,)),
        dma((4,)),
        dma((4,)),
        dma((CHUNKS,)),
        dma((CHUNKS,)),
        dma,
        pltpu.SemaphoreType.REGULAR,
        pltpu.SemaphoreType.REGULAR((3,)),
    ]
    anywhere = pl.BlockSpec(memory_space=pl.ANY)
    return pl.pallas_call(
        kernel,
        out_shape=pltpu.VMEM((ROWS, D), BF),
        in_specs=[anywhere] * 4,
        out_specs=pl.BlockSpec(memory_space=pltpu.VMEM),
        scratch_shapes=scratch,
        compiler_params=pltpu.CompilerParams(
            collective_id=0, has_side_effects=True, vmem_limit_bytes=56 << 20
        ),
        cost_estimate=pl.CostEstimate(flops=1 << 30, bytes_accessed=4 << 20, transcendentals=1 << 21),
    )(queries, keys, values, out_weight)


def solution(mesh):
    rows = P(("batch", "seq"), None)
    return jax.shard_map(
        local, mesh=mesh, in_specs=(rows, rows, rows, P()), out_specs=rows, check_vma=False
    )
```

```python
import math

import jax
import jax.numpy as jnp
from jax import lax
from jax.experimental import pallas as pl
from jax.experimental.pallas import tpu as pltpu
from jax.sharding import PartitionSpec as P

MESH = pl.DeviceIdType.MESH
ROWS = 256
BLOCK = 128
D = 1024
HALF = 512
LANES = 128
CHUNKS = 4
FACTOR = math.log2(math.e) / 8.0
BF, F32 = jnp.bfloat16, jnp.float32
MASKED = -1e30


def averaging(rows):
    i = lax.broadcasted_iota(jnp.int32, (rows // 2, rows), 0)
    j = lax.broadcasted_iota(jnp.int32, (rows // 2, rows), 1)
    return jnp.where((j == 2 * i) | (j == 2 * i + 1), 0.5, 0.0).astype(BF)


def coarsen(x):
    rows = x.shape[0]
    if rows > 256:
        return jnp.concatenate([coarsen(x[i : i + 256]) for i in range(0, rows, 256)], axis=0)
    return jnp.dot(averaging(rows), x, preferred_element_type=F32).astype(BF)


def low_lanes(rows):
    return lax.broadcasted_iota(jnp.int32, (rows, LANES), 1) < 64


def split_keys(k):
    low, zero = low_lanes(k.shape[0]), jnp.zeros_like(k)
    return jnp.where(low, k, zero), jnp.where(low, zero, k)


def split_values(v):
    low, zero, one = low_lanes(v.shape[0]), jnp.zeros_like(v), jnp.ones_like(v)
    return (
        jnp.concatenate([jnp.where(low, v, zero), jnp.where(low, one, zero)], axis=1),
        jnp.concatenate([jnp.where(low, zero, v), jnp.where(low, zero, one)], axis=1),
    )


def scored(q, keys, values, hidden=None):
    scores = []
    for k in keys():
        s = lax.dot_general(q(), k, (((1,), (1,)), ((), ())), preferred_element_type=F32)
        if hidden is not None:
            first, last, masked = hidden
            parts = [s[:, :first], jnp.where(masked, MASKED, s[:, first:last]), s[:, last:]]
            s = jnp.concatenate([part for part in parts if part.shape[1]], axis=1)
        scores.append(s)
    return scores


def weighted(scores):
    weights, peaks = [], []
    for s in scores:
        peak = jnp.max(s, axis=1, keepdims=True)
        weights.append(jnp.exp2((s - peak) * FACTOR).astype(BF))
        peaks.append(peak * FACTOR)
    return jnp.concatenate(weights, axis=1), jnp.where(low_lanes(scores[0].shape[0]), peaks[0], peaks[1])


def summed(weights, peak, values):
    total = jnp.dot(weights, jnp.concatenate(values, axis=0), preferred_element_type=F32)
    return peak, total[:, LANES:], total[:, :LANES]


def attend(units, done=None):
    scores, weights, results = {}, {}, []
    for step in range(len(units) + 3):
        if step < len(units):
            scores[step] = scored(*units[step])
        if 0 <= step - 2 < len(units):
            weights[step - 2] = weighted(scores.pop(step - 2))
        if step >= 3:
            result = summed(*weights.pop(step - 3), units[step - 3][2]())
            results.append(result if done is None else done(step - 3, result))
    return results


def merge(a, b):
    peak = jnp.maximum(a[0], b[0])
    scale_a, scale_b = jnp.exp2(a[0] - peak), jnp.exp2(b[0] - peak)
    return peak, scale_a * a[1] + scale_b * b[1], scale_a * a[2] + scale_b * b[2]


def kernel(q_hbm, k_hbm, v_hbm, w_hbm, out_ref, *scratch):
    (own, qp, kx, vx, wv, st4, r4, z4s, z5s, z6s, z4r, z5r, z6r, cos, cor, s2, r2, s3, r3, ab, ret, acc, rep, held, kv1, k0s, v0s,
     own_sem, pair_sem, w_sem, e1s, e1r, nats, natr, rels, relr, s2s, s2r, s3s, s3r, a2as, a2ar, zs, zr, cs, cr,
     rs, rr, self_sem, plane_sem, z_sem) = scratch
    b, s = lax.axis_index("batch"), lax.axis_index("seq")
    h, x, z, p = s % 2, (s // 2) % 4, s // 8, s // 2
    me8 = s % 8
    partner = (b, p * 2 + 1 - h)

    def pair(index):
        return (b, index * 2 + h)

    def in_plane(x2):
        return (b, z * 8 + x2 * 2 + h)

    def along_z(z2):
        return (b, z2 * 8 + me8)

    def flip(v, bits):
        for bit in (1, 2, 4):
            if bits & bit:
                v = v + bit - 2 * bit * ((v // bit) % 2)
        return v

    def remote(src, dst, ssem, rsem, target):
        return pltpu.make_async_remote_copy(
            src_ref=src, dst_ref=dst, send_sem=ssem, recv_sem=rsem, device_id=target, device_id_type=MESH
        )

    sent = []

    def send(*args):
        copy = remote(*args)
        copy.start()
        sent.append(copy)

    def received(dst, ssem, rsem):
        remote(dst, dst, ssem, rsem, partner).wait_recv()

    def signal(sem, target):
        pl.semaphore_signal(sem, inc=1, device_id=target, device_id_type=MESH)

    def signal_up(sem, far):
        @pl.when(z < 8 - far)
        def _():
            signal(sem, along_z(z + far))

    def signal_down(sem, far):
        @pl.when(z >= far)
        def _():
            signal(sem, along_z(z - far))

    def wait_up(sem, far):
        @pl.when(z >= far)
        def _():
            pl.semaphore_wait(sem, 1)

    def wait_down(sem, far):
        @pl.when(z < 8 - far)
        def _():
            pl.semaphore_wait(sem, 1)

    barrier = pltpu.get_barrier_semaphore()
    signal(barrier, partner)
    for j in range(1, 4):
        signal(barrier, in_plane((x + j) % 4))
    signal_up(barrier, 1)
    signal_down(barrier, 1)

    inputs = (q_hbm, k_hbm, v_hbm)
    own_copies = [pltpu.make_async_copy(inputs[i], own.at[i], own_sem.at[i]) for i in range(3)]
    for copy in own_copies:
        copy.start()

    def mine(c):
        return pl.ds(pl.multiple_of(h * HALF + c * LANES, LANES), LANES)

    def theirs(c):
        return pl.ds(pl.multiple_of((1 - h) * HALF + c * LANES, LANES), LANES)

    def at(start, size):
        return pl.ds(pl.multiple_of(start, 128), size)

    pair_refs = (qp, kx, vx)
    offsets = (0, BLOCK, BLOCK)
    pair_copies = []
    for c in range(CHUNKS):
        for i in range(3):
            copy = pltpu.make_async_copy(
                inputs[i].at[:, mine(c)], pair_refs[i].at[c, at(offsets[i] + ROWS * h, ROWS)], pair_sem.at[c, i]
            )
            copy.start()
            pair_copies.append(copy)
    w_copy = pltpu.make_async_copy(w_hbm, wv, w_sem)
    w_copy.start()

    def exchange_copy(c, i):
        return remote(
            inputs[i].at[:, theirs(c)],
            pair_refs[i].at[c, at(offsets[i] + ROWS * h, ROWS)],
            e1s.at[c, i],
            e1r.at[c, i],
            partner,
        )

    def exchange(c, i):
        copy = exchange_copy(c, i)
        copy.start()
        sent.append(copy)

    def exchanged(c, i):
        received(pair_refs[i].at[c, at(offsets[i] + ROWS * (1 - h), ROWS)], e1s.at[c, i], e1r.at[c, i])

    def level4():
        for i in range(3):
            own_copies[i].wait()
        coarse = [own[i] for i in range(3)]
        for _ in range(4):
            coarse = [coarsen(level) for level in coarse]
        for i in range(3):
            for hp in range(8):
                st4[(hp % 4) * 2 + hp // 4, i] = coarse[i][:, hp * LANES : (hp + 1) * LANES]

    def level4_spread():
        pl.semaphore_wait(plane_sem, 1)
        for j in range(1, 8):
            t = (me8 + j) % 8
            send(
                st4.at[t], r4.at[:, pl.ds(pl.multiple_of(me8 * 16, 16), 16)], a2as.at[t], a2ar.at[me8], (b, z * 8 + t)
            )
        self_copy.start()

    self_copy = pltpu.make_async_copy(st4.at[me8], r4.at[:, pl.ds(pl.multiple_of(me8 * 16, 16), 16)], self_sem)

    native_pair, relay_pair = p - 1 + 2 * h, p + 1 - 2 * h
    native_there = (native_pair >= 0) & (native_pair <= 31)
    relay_there = (relay_pair >= 0) & (relay_pair <= 31)

    def native_rim(c, i):
        return remote(
            inputs[i].at[at(BLOCK * h, BLOCK), mine(c)],
            pair_refs[i].at[c, at(640 * (1 - h), BLOCK)],
            nats.at[c, i - 1],
            natr.at[c, i - 1],
            pair(native_pair),
        )

    def relay_rim(c, i):
        return remote(
            pair_refs[i].at[c, at(BLOCK * (4 - 3 * h), BLOCK)],
            pair_refs[i].at[c, at(640 * h, BLOCK)],
            rels.at[c, i - 1],
            relr.at[c, i - 1],
            pair(relay_pair),
        )

    def native_rims(c):
        @pl.when(native_there)
        def _():
            for i in (1, 2):
                native_rim(c, i).start()

    def rims_received(c):
        @pl.when(relay_there)
        def _():
            for i in (1, 2):
                received(pair_refs[i].at[c, at(640 * (1 - h), BLOCK)], nats.at[c, i - 1], natr.at[c, i - 1])

        @pl.when(native_there)
        def _():
            for i in (1, 2):
                received(pair_refs[i].at[c, at(640 * h, BLOCK)], rels.at[c, i - 1], relr.at[c, i - 1])

    def rims_sent():
        @pl.when(native_there)
        def _():
            for c in range(CHUNKS):
                for i in (1, 2):
                    native_rim(c, i).wait_send()

        @pl.when(relay_there)
        def _():
            for c in range(CHUNKS):
                for i in (1, 2):
                    relay_rim(c, i).wait_send()

    def no_rims():
        @pl.when(p == 0)
        def _():
            for ref in (kx, vx):
                ref[:, :BLOCK] = jnp.zeros((CHUNKS, BLOCK, LANES), BF)

        @pl.when(p == 31)
        def _():
            for ref in (kx, vx):
                ref[:, 640:] = jnp.zeros((CHUNKS, BLOCK, LANES), BF)

    def spread(c):
        for i in (1, 2):
            pair_copies[c * 3 + i].wait()
            exchanged(c, i)

        @pl.when(relay_there)
        def _():
            for i in (1, 2):
                relay_rim(c, i).start()

        fine = jnp.concatenate([kx[c, BLOCK : BLOCK + 512], vx[c, BLOCK : BLOCK + 512]], axis=1)
        level1 = coarsen(fine)
        level2 = coarsen(level1)
        level3 = coarsen(level2)
        for i in range(2):
            side = slice(LANES * i, LANES * i + LANES)
            s2[c, i] = level2[:, side]
            s3[c, i] = level3[:, side]
            kv1[c, i] = level1[:, side]
        send(s2.at[c], r2.at[c], s2s.at[c], s2r.at[c], in_plane(flip(x, 1)))
        for k in (0, 1):
            send(
                s3.at[c], r3.at[c, :, pl.ds(64 * k, 64)], s3s.at[c, k], s3r.at[c, k], in_plane(flip(x, 2 + k))
            )

    def coarse_spread():
        self_copy.wait()
        for j in range(1, 8):
            t = (me8 + j) % 8
            received(r4.at[:, pl.ds(pl.multiple_of(t * 16, 16), 16)], a2as.at[t], a2ar.at[t])
        for i in (1, 2):
            level4 = r4[i]
            level5 = coarsen(level4)
            z4s[i - 1] = level4
            z5s[i - 1] = level5
            z6s[i - 1] = coarsen(level5)
        for copy in near_copies():
            copy.start()

    def near_copies():
        return [remote(z4s, z4r, zs.at[0], zr.at[0], along_z(flip(z, 1)))] + [
            remote(z5s, z5r.at[:, pl.ds(64 * k, 64)], zs.at[1 + k], zr.at[1 + k], along_z(flip(z, 2 + k)))
            for k in range(2)
        ]

    def far_copies():
        return [
            remote(z6s, z6r.at[:, pl.ds(32 * k, 32)], zs.at[3 + k], zr.at[3 + k], along_z(flip(z, 4 + k)))
            for k in range(4)
        ]

    def coarse_far():
        for copy in far_copies():
            copy.start()

    def coarse_late_planes():
        wait_up(z_sem.at[2], 4)
        coarse_spread()
        coarse_far()

    def coarse_early_planes():
        coarse_spread()

    def coarse_far_early_planes():
        wait_down(z_sem.at[5], 4)
        pl.when(z < 4)(coarse_far)

    def repeated(level):
        rows = level[0].shape[0]
        for i in range(3):
            rep[i, pl.ds(0, rows, stride=2), :] = level[i]
            rep[i, pl.ds(1, rows, stride=2), :] = level[i]
        return tuple(rep[i, : 2 * rows, :] for i in range(3))

    def coarse_attend():
        received(z4r, zs.at[0], zr.at[0])
        for k in range(2):
            received(z5r.at[:, pl.ds(64 * k, 64)], zs.at[1 + k], zr.at[1 + k])
        for k in range(4):
            received(z6r.at[:, pl.ds(32 * k, 32)], zs.at[3 + k], zr.at[3 + k])
        q4 = r4[0]
        q5 = coarsen(q4)
        q6 = coarsen(q5)
        level, level5, level4 = attend([
            (lambda q=q, r=r: q, lambda r=r: split_keys(r[0]), lambda r=r: split_values(r[1]))
            for q, r in ((q6, z6r), (q5, z5r), (q4, z4r))
        ])
        level = merge(repeated(level), level5)
        level = merge(repeated(level), level4)
        for i in range(3):
            for x2 in range(4):
                cos[x2, i] = level[i][x2 * 32 : x2 * 32 + 32]
        for j in range(1, 4):
            x2 = (x + j) % 4
            send(cos.at[x2], cor.at[x], cs.at[x2], cr.at[x], in_plane(x2))
        local = pltpu.make_async_copy(cos.at[x], cor.at[x], self_sem)
        local.start()
        local.wait()

    def coarse_received():
        for j in range(1, 4):
            x2 = (x + j) % 4
            received(cor.at[x2], cs.at[x2], cr.at[x2])

    def give_back(c):
        send(ab.at[c, at(ROWS * (1 - h), ROWS)], ret.at[c], rs.at[c], rr.at[c], partner)

    def windows(c, deferred):
        pair_copies[c * 3].wait()
        exchanged(c, 0)
        rims_received(c)
        received(r2.at[c], s2s.at[c], s2r.at[c])
        for k in (0, 1):
            received(r3.at[c, :, pl.ds(64 * k, 64)], s3s.at[c, k], s3r.at[c, k])
        q0 = qp[c]
        q1 = coarsen(q0)
        q2 = coarsen(q1)
        q3 = coarsen(q2)
        for head, (k0, v0) in enumerate(zip(split_keys(kx[c]), split_values(vx[c]))):
            k0s[head] = k0
            v0s[head] = v0
        k1 = split_keys(kv1[c, 0])
        v1 = split_values(kv1[c, 1])

        def block_of(unit):
            return (2 * (1 - h), 2 * (1 - h) + 1, 2 * h, 2 * h + 1)[unit]

        def fine_unit(unit):
            block = block_of(unit)
            start = BLOCK * block
            hidden = ((0, 128, (p == 0) & (block == 0)), (256, 384, (p == 31) & (block == 3)))[unit % 2]
            return (
                lambda: qp[c, at(start, BLOCK)],
                lambda: [k0s[0, at(start, 384)], k0s[1, at(start, 384)]],
                lambda: [v0s[0, at(start, 384)], v0s[1, at(start, 384)]],
                hidden,
            )

        def sibling_unit(block):
            other = slice(128 * (1 - block), 128 * (2 - block))
            return (
                lambda: q1[128 * block : 128 * block + 128],
                lambda: [k[other] for k in k1],
                lambda: [v[other] for v in v1],
            )

        units = [
            (lambda: q3, lambda: split_keys(r3[c, 0]), lambda: split_values(r3[c, 1])),
            (lambda: q2, lambda: split_keys(r2[c, 0]), lambda: split_values(r2[c, 1])),
            sibling_unit(0),
            sibling_unit(1),
        ] + [fine_unit(unit) for unit in range(4)]
        state = {}

        def done(index, result):
            if index == 0:
                if not deferred:
                    result = merge(repeated(tuple(cor[c, i] for i in range(3))), result)
                state["level"] = result
            elif index == 1:
                state["level"] = merge(repeated(state["level"]), result)
            elif index == 2:
                state["half"] = result
            elif index == 3:
                both = tuple(jnp.concatenate([state["half"][i], result[i]], axis=0) for i in range(3))
                repeated(merge(repeated(state["level"]), both))
            else:
                rows = at(BLOCK * block_of(index - 4), BLOCK)
                merged = merge(tuple(rep[i, rows] for i in range(3)), result)
                if deferred:
                    for i in range(3):
                        held[c, i, rows] = merged[i]
                else:
                    ab[c, rows] = (merged[2] / merged[1]).astype(BF)
                    if index == 5:
                        give_back(c)

        attend(units, done)

    def late_merge(c, side):
        for i in range(3):
            level = cor[c, i, pl.ds(pl.multiple_of(16 * side, 16), 16)]
            for k in range(16):
                rep[i, pl.ds(k, 16, stride=16), :] = level
        for block in range(2):
            here = slice(BLOCK * block, BLOCK * block + BLOCK)
            rows = at(ROWS * side + BLOCK * block, BLOCK)
            _, mass, summary = merge(tuple(rep[i, here] for i in range(3)), tuple(held[c, i, rows] for i in range(3)))
            ab[c, rows] = (summary / mass).astype(BF)

    def meet_next_planes():
        wait_up(z_sem.at[0], 1)
        wait_down(z_sem.at[3], 1)
        signal_up(z_sem.at[1], 2)
        signal_down(z_sem.at[4], 2)

    def meet_far_planes():
        wait_up(z_sem.at[1], 2)
        wait_down(z_sem.at[4], 2)
        signal_up(z_sem.at[2], 4)
        signal_down(z_sem.at[5], 4)

    no_rims()
    pl.semaphore_wait(barrier, 4 + jnp.where(z >= 1, 1, 0) + jnp.where(z < 7, 1, 0))
    signal(plane_sem, partner)
    signal_up(z_sem.at[0], 1)
    signal_down(z_sem.at[3], 1)
    exchange(0, 1)
    first_values = exchange_copy(0, 2)
    sent.append(first_values)
    pl.when(z < 4)(first_values.start)
    level4()
    level4_spread()
    pl.when(z >= 4)(first_values.start)
    for c, i in ((1, 1), (1, 2), (0, 0), (2, 1), (2, 2), (3, 1), (3, 2), (1, 0), (2, 0), (3, 0)):
        exchange(c, i)
    meet_next_planes()
    native_rims(0)
    meet_far_planes()
    pl.when(z >= 4)(coarse_late_planes)
    spread(0)
    native_rims(1)
    pl.when(z < 4)(coarse_early_planes)
    spread(1)
    native_rims(2)
    coarse_far_early_planes()
    windows(0, True)
    spread(2)
    coarse_attend()
    native_rims(3)
    spread(3)
    windows(1, True)
    windows(2, True)
    coarse_received()
    late_merge(0, 1 - h)
    give_back(0)
    late_merge(1, 1 - h)
    give_back(1)
    late_merge(2, 1 - h)
    give_back(2)
    windows(3, False)
    late_merge(0, h)
    late_merge(1, h)
    late_merge(2, h)

    def finish():
        for copy in sent + near_copies() + far_copies():
            copy.wait_send()
        rims_sent()

    w_copy.wait()
    for c in range(CHUNKS):
        part = jnp.dot(
            ab[c, at(ROWS * h, ROWS)], wv[at(HALF * h + LANES * c, LANES)], preferred_element_type=F32
        )
        if c == 0:
            acc[...] = part
        else:
            acc[...] += part
    for c in range(CHUNKS):
        received(ret.at[c], rs.at[c], rr.at[c])
        weight = wv[at(HALF * (1 - h) + LANES * c, LANES)]
        if c < CHUNKS - 1:
            acc[...] += jnp.dot(ret[c], weight, preferred_element_type=F32)
        else:
            for i in range(4):
                rows = slice(64 * i, 64 * i + 64)
                part = jnp.dot(ret[c, rows], weight, preferred_element_type=F32)
                out_ref[rows] = (acc[rows] + part).astype(BF)
    finish()


def local(queries, keys, values, out_weight):
    vmem = pltpu.VMEM
    dma = pltpu.SemaphoreType.DMA
    scratch = [
        vmem((3, ROWS, D), BF),
        vmem((CHUNKS, 512, LANES), BF),
        vmem((CHUNKS, 768, LANES), BF),
        vmem((CHUNKS, 768, LANES), BF),
        vmem((D, D), BF),
        vmem((8, 3, 16, LANES), BF),
        vmem((3, 128, LANES), BF),
        vmem((2, 128, LANES), BF),
        vmem((2, 64, LANES), BF),
        vmem((2, 32, LANES), BF),
        vmem((2, 128, LANES), BF),
        vmem((2, 128, LANES), BF),
        vmem((2, 128, LANES), BF),
        vmem((4, 3, 32, LANES), F32),
        vmem((4, 3, 32, LANES), F32),
        vmem((CHUNKS, 2, 128, LANES), BF),
        vmem((CHUNKS, 2, 128, LANES), BF),
        vmem((CHUNKS, 2, 64, LANES), BF),
        vmem((CHUNKS, 2, 128, LANES), BF),
        vmem((CHUNKS, 512, LANES), BF),
        vmem((CHUNKS, ROWS, LANES), BF),
        vmem((ROWS, D), F32),
        vmem((3, 512, LANES), F32),
        vmem((CHUNKS, 3, 512, LANES), F32),
        vmem((CHUNKS, 2, 256, LANES), BF),
        vmem((2, 768, LANES), BF),
        vmem((2, 768, 2 * LANES), BF),
        dma((3,)),
        dma((CHUNKS, 3)),
        dma,
        dma((CHUNKS, 3)),
        dma((CHUNKS, 3)),
        dma((CHUNKS, 2)),
        dma((CHUNKS, 2)),
        dma((CHUNKS, 2)),
        dma((CHUNKS, 2)),
        dma((CHUNKS,)),
        dma((CHUNKS,)),
        dma((CHUNKS, 2)),
        dma((CHUNKS, 2)),
        dma((8,)),
        dma((8,)),
        dma((7,)),
        dma((7,)),
        dma((4,)),
        dma((4,)),
        dma((CHUNKS,)),
        dma((CHUNKS,)),
        dma,
        pltpu.SemaphoreType.REGULAR,
        pltpu.SemaphoreType.REGULAR((6,)),
    ]
    anywhere = pl.BlockSpec(memory_space=pl.ANY)
    return pl.pallas_call(
        kernel,
        out_shape=pltpu.VMEM((ROWS, D), BF),
        in_specs=[anywhere] * 4,
        out_specs=pl.BlockSpec(memory_space=pltpu.VMEM),
        scratch_shapes=scratch,
        compiler_params=pltpu.CompilerParams(
            collective_id=0, has_side_effects=True, vmem_limit_bytes=56 << 20
        ),
        cost_estimate=pl.CostEstimate(flops=1 << 30, bytes_accessed=4 << 20, transcendentals=1 << 21),
    )(queries, keys, values, out_weight)


def solution(mesh):
    rows = P(("batch", "seq"), None)
    return jax.shard_map(
        local, mesh=mesh, in_specs=(rows, rows, rows, P()), out_specs=rows, check_vma=False
    )
```
